512 devices in a mesh: blk: 8 (over z_lo, core), aux: 64 (over z_hi, x, y).
Axes of the slice: x: 4, y: 4, z: 16 (z_hi: 4, z_lo: 4; z = z_hi * 4 + z_lo), core: 2. Of those that a mesh axis runs over, the one named last changes fastest.
Arguments:
- three_index: bfloat16 [12800, 16, 4096], P('aux', 'blk'), may hold values from -1 to 1
- occ_energy: float32 [16], replicated, may hold values from -1.5 to -0.4
- vir_energy: float32 [4096], replicated, may hold values from 0.2 to 2.5
Outputs:
- vv_density: float32 [768, 96], P('blk')
- oo_density: float32 [16, 2], P('blk')
The draws below stay inside these ranges and needn't reach their ends.
All inputs are finite; a program needn't handle non-finite values.
Results may differ from the reference program's by a relative error of at most 0.00055.
Values may be sent and summed in bfloat16 or wider, within the bound.
A program may use at most 64 MiB of HBM per device.

```python
import jax
import jax.numpy as jnp
from jax import lax

NAUX = 12800
V = 4096
OB = 2
AW = 96
NOCC = 16
N_BLK = 8


def draw_three_index(key, part):
    key = jax.random.fold_in(key, 7)
    pairs = 3 * OB * OB - OB
    target = (0.25 / (4.0 * pairs * V)) ** 0.5
    factor = (3.5 * target / NAUX ** 0.5) ** 0.5
    values = jnp.clip(jax.random.normal(key, (NAUX, NOCC, V), jnp.float32), -4.0, 4.0)
    return (values * factor).astype(jnp.bfloat16)


def setup_inputs(seed: int = 0) -> dict:
    streams_of = jax.random.split(jax.random.key(seed), 4)
    return {
        "three_index": draw_three_index(jax.random.fold_in(streams_of[3], 71), 0),
        "occ_energy": jnp.clip(jax.random.uniform(streams_of[1], (NOCC,), jnp.float32, -1.5, -0.4), -1.5, -0.4),
        "vir_energy": jnp.clip(jax.random.uniform(streams_of[2], (V,), jnp.float32, 0.2, 2.5), 0.2, 2.5),
    }


def amplitude(kmat, row_energy, col_energy, win_energy, tile_energy):
    denom = row_energy[:, None, None, None] + col_energy[None, None, :, None] - win_energy[None, :, None, None] - tile_energy[None, None, None, :]
    return kmat / denom


def own_terms(t_own):
    tt_own = 2.0 * t_own - jnp.transpose(t_own, (2, 1, 0, 3))
    vv_part = jnp.einsum("iajb,icjb->ac", t_own, tt_own)
    oo_part = jnp.einsum("iakb,jakb->ij", t_own, tt_own)
    return vv_part, oo_part


def cross_terms(t_op, t_po):
    tt_op = 2.0 * t_op - jnp.transpose(t_po, (2, 1, 0, 3))
    tt_po = 2.0 * t_po - jnp.transpose(t_op, (2, 1, 0, 3))
    vv_part = jnp.einsum("iajb,icjb->ac", t_op, tt_op) + jnp.einsum("iajb,icjb->ac", t_po, tt_po)
    oo_part = jnp.einsum("iakb,jakb->ij", t_op, tt_op)
    return vv_part, oo_part


def reference(three_index, occ_energy, vir_energy):
    win_energy = vir_energy[:AW]
    seq = jnp.arange(OB, dtype=jnp.int32)
    offdiag = (seq[:, None] != seq[None, :]).astype(jnp.float32)

    def product(left, right):
        slab = left[:, :, :AW].reshape(NAUX, OB * AW)
        whole = right.reshape(NAUX, OB * V)
        return jnp.dot(slab.T, whole, preferred_element_type=jnp.float32).reshape(OB, AW, OB, V)

    def one_group(block_index):
        prev_index = (block_index + N_BLK - 1) % N_BLK
        start_own = (block_index * OB).astype(jnp.int32)
        start_prev = (prev_index * OB).astype(jnp.int32)
        own_rows = lax.dynamic_slice_in_dim(three_index, start_own, OB, 1)
        prev_rows = lax.dynamic_slice_in_dim(three_index, start_prev, OB, 1)
        e_own = lax.dynamic_slice_in_dim(occ_energy, start_own, OB, 0)
        e_prev = lax.dynamic_slice_in_dim(occ_energy, start_prev, OB, 0)
        t_own = amplitude(product(own_rows, own_rows), e_own, e_own, win_energy, vir_energy) * offdiag[:, None, :, None]
        t_op = amplitude(product(own_rows, prev_rows), e_own, e_prev, win_energy, vir_energy)
        t_po = amplitude(product(prev_rows, own_rows), e_prev, e_own, win_energy, vir_energy)
        vv_own, oo_own = own_terms(t_own)
        vv_cross, oo_cross = cross_terms(t_op, t_po)
        return 2.0 * (vv_own + vv_cross), -2.0 * (oo_own + oo_cross)

    vv_all, oo_all = lax.map(one_group, jnp.arange(N_BLK, dtype=jnp.int32))
    return vv_all.reshape(N_BLK * AW, AW), oo_all.reshape(NOCC, OB)
```

```python
import functools

import jax
import jax.numpy as jnp
from jax import lax
from jax.experimental import pallas as pl
from jax.experimental.pallas import tpu as pltpu
from jax.sharding import PartitionSpec as P

MESH = pl.DeviceIdType.MESH
AW = 96
LANE = 128
CHUNKS = 4
TILES = 2
N = 4
WIDE = 1024
OPW = 4 * AW
RESTW = WIDE - OPW
LINK = jnp.bfloat16
F32 = jnp.float32


def spread(raw):
    rows = lax.broadcasted_iota(jnp.int32, raw.shape, 0)
    even = lax.rem(rows, 2) == 0
    zero = jnp.zeros_like(raw)
    up = jnp.concatenate([raw[1:], raw[:1]], axis=0)
    down = jnp.concatenate([raw[-1:], raw[:-1]], axis=0)
    f00 = jnp.where(even, raw, zero)
    f11 = jnp.where(even, zero, raw)
    f10 = jnp.where(even, up, zero)
    f01 = jnp.where(even, zero, down)
    return [f[:, :AW] for f in (f00, f01, f10, f11)]


def kernel(
    x_ref, occ_ref, vir_ref, vv_ref, oo_ref,
    xb, sl, sw, pb, yb, sb, zop, zrest, tb, va, vb, vc, vd,
    loc_sem, xs, xr, ss, sr, ys, yr, os_, or_, rs, rr, vs, vr,
):
    g = lax.axis_index("blk")
    aux = lax.axis_index("aux")
    blocks = 8
    zh = aux // 16
    x = lax.rem(aux // 4, 4)
    y = lax.rem(aux, 4)
    nxt, prv = lax.rem(g + 1, blocks), lax.rem(g + blocks - 1, blocks)
    depth = x_ref.shape[0]
    rows = 2 * depth

    def at(z_, x_, y_, g_=None):
        return {"blk": g if g_ is None else g_, "aux": z_ * 16 + x_ * 4 + y_}

    def go(v, d):
        return lax.rem(v + d, N)

    peers = [at(zh, go(x, d), y) for d in (1, 2, 3)]
    peers += [at(zh, x, go(y, d)) for d in (1, 2, 3)]
    peers += [at(go(zh, d), x, y) for d in (1, 2, 3)]
    peers += [at(go(zh, d), x, y, h) for h in (nxt, prv) for d in (0, 1, 2, 3)]
    barrier = pltpu.get_barrier_semaphore()
    for peer in peers:
        pl.semaphore_signal(barrier, inc=1, device_id=peer, device_id_type=MESH)
    pl.semaphore_wait(barrier, len(peers))

    def remote(src, dst, send, recv, peer):
        return pltpu.make_async_remote_copy(
            src_ref=src, dst_ref=dst, send_sem=send, recv_sem=recv, device_id=peer, device_id_type=MESH
        )

    sends = []
    own_slab = pltpu.make_async_copy(x_ref.at[:, 0], sl.at[0, 0], loc_sem.at[0])
    own_slab.start()
    slab_x = []
    for d in (1, 2, 3):
        c = remote(x_ref.at[:, 0], sl.at[0, d], ss.at[0, d], sr.at[0, d], at(zh, go(x, d), y))
        c.start()
        slab_x.append(c)

    def forward(src, d):
        out = []
        for group, h in ((2, nxt), (1, prv)):
            c = remote(src, sl.at[group, d], ss.at[group, d], sr.at[group, d], at(zh, x, y, h))
            c.start()
            out.append(c)
        return out

    slab_f = forward(x_ref.at[:, 0], 0)

    tiles = {}
    locals_ = {}
    for c in range(CHUNKS):
        for l in range(TILES):
            for d in (1, 2, 3):
                lt = (c * N + go(x, d)) * TILES + l
                cp = remote(
                    x_ref.at[:, lt], xb.at[c, l, d], xs.at[c, l, d], xr.at[c, l, d], at(zh, go(x, d), y)
                )
                cp.start()
                tiles[c, l, d] = cp
            lt = (c * N + x) * TILES + l
            cp = pltpu.make_async_copy(x_ref.at[:, lt], xb.at[c, l, 0], loc_sem.at[1 + c * TILES + l])
            cp.start()
            locals_[c, l] = cp

    own_slab.wait()
    for d in (1, 2, 3):
        slab_x[d - 1].wait_recv()
        slab_f += forward(sl.at[0, d], d)

    for cp in slab_f:
        cp.wait_recv()
    for d in range(N):
        own = spread(sl.at[0, d].reshape(rows, LANE)[...].astype(F32))
        nex = spread(sl.at[1, d].reshape(rows, LANE)[...].astype(F32))
        pre = spread(sl.at[2, d].reshape(rows, LANE)[...].astype(F32))
        pad = jnp.zeros((rows, WIDE - 10 * AW), F32)
        sw[pl.ds(d * rows, rows), :] = jnp.concatenate(nex + pre + [own[1], own[2], pad], axis=1).astype(jnp.bfloat16)

    per = TILES * LANE // N
    fin = per // N
    y_copies, z_copies, z_local = {}, {}, {}

    def multiply(c):
        for l in range(TILES):
            for d in (1, 2, 3):
                tiles[c, l, d].wait_recv()
            locals_[c, l].wait()
            block = xb.at[c, l].reshape(N * rows, LANE)[...]
            prod = lax.dot_general(block, sw[...], (((0,), (0,)), ((), ())), preferred_element_type=F32)
            pb[c, pl.ds(l * LANE, LANE), :] = prod.astype(LINK)
        for d in (1, 2, 3):
            yy = go(y, d)
            cp = remote(
                pb.at[c, pl.ds(pl.multiple_of(yy * per, per), per)], yb.at[c, d - 1],
                ys.at[c, d - 1], yr.at[c, d - 1], at(zh, x, yy),
            )
            cp.start()
            y_copies[c, d] = cp

    def reduce_y(c):
        for d in (1, 2, 3):
            y_copies[c, d].wait_recv()
        total = pb[c, pl.ds(pl.multiple_of(y * per, per), per), :].astype(F32)
        for d in range(3):
            total = total + yb[c, d].astype(F32)
        sb[c] = total.astype(LINK)
        for d in range(N):
            zz = go(zh, d)
            part = pl.ds(pl.multiple_of(zz * fin, fin), fin)
            cp = remote(
                sb.at[c, part, pl.ds(0, OPW)], zop.at[c, d], os_.at[c, d], or_.at[c, d], at(zz, x, y, nxt)
            )
            cp.start()
            z_copies[c, d, 0] = cp
            if d == 0:
                cp = pltpu.make_async_copy(
                    sb.at[c, part, pl.ds(OPW, RESTW)], zrest.at[c, d], rr.at[c, d]
                )
                cp.start()
                z_local[c] = cp
            else:
                cp = remote(
                    sb.at[c, part, pl.ds(OPW, RESTW)], zrest.at[c, d], rs.at[c, d], rr.at[c, d], at(zz, x, y)
                )
                cp.start()
                z_copies[c, d, 1] = cp

    def reduce_z(c):
        z_local[c].wait()
        for d in range(N):
            z_copies[c, d, 0].wait_recv()
            if d:
                z_copies[c, d, 1].wait_recv()
        first = zop[c, 0].astype(F32)
        second = zrest[c, 0].astype(F32)
        for d in (1, 2, 3):
            first = first + zop[c, d].astype(F32)
            second = second + zrest[c, d].astype(F32)
        tb[pl.ds(c * fin, fin), pl.ds(0, OPW)] = first
        tb[pl.ds(c * fin, fin), pl.ds(OPW, RESTW)] = second

    for step in range(CHUNKS + 2):
        if step < CHUNKS:
            multiply(step)
        if 0 <= step - 1 < CHUNKS:
            reduce_y(step - 1)
        if 0 <= step - 2 < CHUNKS:
            reduce_z(step - 2)

    lane = lax.broadcasted_iota(jnp.int32, (fin, LANE), 1)
    row = lax.broadcasted_iota(jnp.int32, (fin, LANE), 0)
    offset = lax.rem(y, 2) * per + zh * fin
    columns = []
    for c in range(CHUNKS):
        lt = (c * N + x) * TILES + y // 2
        line = jnp.broadcast_to(vir_ref[pl.ds(lt, 1), :], (fin, LANE))
        columns.append(jnp.sum(jnp.where(lane == row + offset, line, 0.0), axis=1, keepdims=True))
    eb = jnp.concatenate(columns, axis=0)
    ea = vir_ref[0:1, 0:AW]
    eo = [occ_ref[2 * g], occ_ref[2 * g + 1]]
    ep = [occ_ref[2 * prv], occ_ref[2 * prv + 1]]

    def amplitude(k, ei, ej):
        return tb[:, k * AW:(k + 1) * AW] / (((ei + ej) - ea) - eb)

    op = [[amplitude(2 * i + j, eo[i], ep[j]) for j in range(2)] for i in range(2)]
    po = [[amplitude(4 + 2 * i + j, ep[i], eo[j]) for j in range(2)] for i in range(2)]
    ow = [amplitude(8, eo[0], eo[1]), amplitude(9, eo[1], eo[0])]
    mop = [[2.0 * op[i][j] - po[j][i] for j in range(2)] for i in range(2)]
    mpo = [[2.0 * po[i][j] - op[j][i] for j in range(2)] for i in range(2)]
    mow = [2.0 * ow[0] - ow[1], 2.0 * ow[1] - ow[0]]
    left = jnp.concatenate(op[0] + op[1] + po[0] + po[1] + ow, axis=0)
    right = jnp.concatenate(mop[0] + mop[1] + mpo[0] + mpo[1] + mow, axis=0)
    vv = lax.dot_general(
        left, right, (((0,), (0,)), ((), ())), preferred_element_type=F32, precision=lax.Precision.HIGHEST
    )

    def inner(a, b):
        return jnp.sum(jnp.sum(a * b, axis=1, keepdims=True), axis=0, keepdims=True)

    oo = []
    for i in range(2):
        for j in range(2):
            s = inner(op[i][0], mop[j][0]) + inner(op[i][1], mop[j][1])
            if i == j:
                s = s + inner(ow[i], mow[i])
            oo.append(s)
    corner = jnp.zeros((AW, LANE - AW), F32)
    cl = lax.broadcasted_iota(jnp.int32, corner.shape, 1)
    for k in range(4):
        corner = jnp.where(cl == k, jnp.broadcast_to(oo[k], corner.shape), corner)
    va[...] = jnp.concatenate([2.0 * vv, -2.0 * corner], axis=1)

    piece = AW // N
    fin_copies = []
    group = []
    for d in (1, 2, 3):
        yy = go(y, d)
        cp = remote(
            va.at[pl.ds(pl.multiple_of(yy * piece, 8), piece)], vb.at[d - 1], vs.at[0, d], vr.at[0, d], at(zh, x, yy)
        )
        cp.start()
        group.append(cp)
    for cp in group:
        cp.wait_recv()
    fin_copies += group
    total = va[pl.ds(pl.multiple_of(y * piece, 8), piece), :]
    for d in range(3):
        total = total + vb[d]

    def everyone(total, buf, stage, me, where):
        buf[me] = total
        group = []
        for d in (1, 2, 3):
            cp = remote(buf.at[me], buf.at[me], vs.at[stage, d], vr.at[stage, d], where(d))
            cp.start()
            group.append(cp)
        for cp in group:
            cp.wait_recv()
        return group

    fin_copies += everyone(total, vc.at[0], 1, x, lambda d: at(zh, go(x, d), y))
    total = (vc[0, 0] + vc[0, 1]) + (vc[0, 2] + vc[0, 3])
    fin_copies += everyone(total, vc.at[1], 2, zh, lambda d: at(go(zh, d), x, y))
    total = (vc[1, 0] + vc[1, 1]) + (vc[1, 2] + vc[1, 3])
    fin_copies += everyone(total, vd, 3, y, lambda d: at(zh, x, go(y, d)))
    for k in range(N):
        vv_ref[pl.ds(k * piece, piece), :] = vd[k][:, :AW]
    tail = vd[0][0:1, AW:]
    oo_ref[...] = jnp.concatenate([tail[:, 0:2], tail[:, 2:4]], axis=0)

    for group in (slab_x, slab_f, tiles.values(), y_copies.values(), z_copies.values(), fin_copies):
        for cp in group:
            cp.wait_send()


def shards(three_index, occ_energy, vir_energy):
    depth, occ, vir = three_index.shape
    tiles = vir // LANE
    view = three_index.reshape(depth, occ, tiles, LANE).transpose(0, 2, 1, 3)
    bf16 = jnp.bfloat16
    per = TILES * LANE // N
    fin = per // N
    piece = AW // N
    dma = pltpu.SemaphoreType.DMA
    return pl.pallas_call(
        kernel,
        out_shape=(jax.ShapeDtypeStruct((AW, AW), F32), jax.ShapeDtypeStruct((2, 2), F32)),
        in_specs=[
            pl.BlockSpec(memory_space=pl.ANY),
            pl.BlockSpec(memory_space=pltpu.SMEM),
            pl.BlockSpec(memory_space=pltpu.VMEM),
        ],
        out_specs=(pl.BlockSpec(memory_space=pltpu.VMEM), pl.BlockSpec(memory_space=pltpu.VMEM)),
        scratch_shapes=[
            pltpu.VMEM((CHUNKS, TILES, N, depth, occ, LANE), bf16),
            pltpu.VMEM((3, N, depth, occ, LANE), bf16),
            pltpu.VMEM((N * depth * occ, WIDE), bf16),
            pltpu.VMEM((CHUNKS, TILES * LANE, WIDE), LINK),
            pltpu.VMEM((CHUNKS, 3, per, WIDE), LINK),
            pltpu.VMEM((CHUNKS, per, WIDE), LINK),
            pltpu.VMEM((CHUNKS, N, fin, OPW), LINK),
            pltpu.VMEM((CHUNKS, N, fin, RESTW), LINK),
            pltpu.VMEM((CHUNKS * fin, WIDE), F32),
            pltpu.VMEM((AW, LANE), F32),
            pltpu.VMEM((3, piece, LANE), F32),
            pltpu.VMEM((2, N, piece, LANE), F32),
            pltpu.VMEM((N, piece, LANE), F32),
            dma((1 + CHUNKS * TILES,)),
            dma((CHUNKS, TILES, N)), dma((CHUNKS, TILES, N)),
            dma((3, N)), dma((3, N)),
            dma((CHUNKS, 3)), dma((CHUNKS, 3)),
            dma((CHUNKS, N)), dma((CHUNKS, N)),
            dma((CHUNKS, N)), dma((CHUNKS, N)),
            dma((4, N)), dma((4, N)),
        ],
        compiler_params=pltpu.CompilerParams(
            collective_id=0, has_side_effects=True, vmem_limit_bytes=56 * 1024 * 1024
        ),
        cost_estimate=pl.CostEstimate(flops=4_000_000_000, bytes_accessed=8_000_000, transcendentals=0),
    )(view, occ_energy, vir_energy.reshape(vir // LANE, LANE))


def solution(mesh):
    return jax.shard_map(
        shards,
        mesh=mesh,
        in_specs=(P("aux", "blk", None), P(), P()),
        out_specs=(P("blk", None), P("blk", None)),
        check_vma=False,
    )
```

```python
import functools

import jax
import jax.numpy as jnp
from jax import lax
from jax.experimental import pallas as pl
from jax.experimental.pallas import tpu as pltpu
from jax.sharding import PartitionSpec as P

MESH = pl.DeviceIdType.MESH
AW = 96
LANE = 128
CHUNKS = 8
N = 4
WIDE = 1024
OPW = 4 * AW
RESTW = WIDE - OPW
LINK = jnp.bfloat16
F32 = jnp.float32


def spread(raw):
    rows = lax.broadcasted_iota(jnp.int32, raw.shape, 0)
    even = lax.rem(rows, 2) == 0
    zero = jnp.zeros_like(raw)
    up = jnp.concatenate([raw[1:], raw[:1]], axis=0)
    down = jnp.concatenate([raw[-1:], raw[:-1]], axis=0)
    f00 = jnp.where(even, raw, zero)
    f11 = jnp.where(even, zero, raw)
    f10 = jnp.where(even, up, zero)
    f01 = jnp.where(even, zero, down)
    return [f[:, :AW] for f in (f00, f01, f10, f11)]


def kernel(
    x_ref, occ_ref, vir_ref, out_ref,
    xb, sl, sw, pb, yb, sb, zop, zrest, tb, va, vb, vc, vd,
    loc_sem, xs, xr, ss, sr, ys, yr, os_, or_, rs, rr, vs, vr,
):
    g = lax.axis_index("blk")
    aux = lax.axis_index("aux")
    blocks = 8
    zh = aux // 16
    x = lax.rem(aux // 4, 4)
    y = lax.rem(aux, 4)
    nxt, prv = lax.rem(g + 1, blocks), lax.rem(g + blocks - 1, blocks)
    depth = x_ref.shape[0]
    rows = 2 * depth

    def at(z_, x_, y_, g_=None):
        return {"blk": g if g_ is None else g_, "aux": z_ * 16 + x_ * 4 + y_}

    def go(v, d):
        return lax.rem(v + d, N)

    peers = [at(go(zh, d), x, y, h) for d in (2, 1, 3) for h in (nxt, prv, g)]
    peers += [at(zh, go(x, d), y) for d in (2, 1, 3)]
    peers += [at(zh, x, go(y, d)) for d in (2, 1, 3)]
    peers += [at(zh, x, y, h) for h in (nxt, prv)]
    barrier = pltpu.get_barrier_semaphore()
    for peer in peers:
        pl.semaphore_signal(barrier, inc=1, device_id=peer, device_id_type=MESH)
    pl.semaphore_wait(barrier, len(peers))

    def remote(src, dst, send, recv, peer):
        return pltpu.make_async_remote_copy(
            src_ref=src, dst_ref=dst, send_sem=send, recv_sem=recv, device_id=peer, device_id_type=MESH
        )

    place = (x, y)

    def along(axis, d):
        return at(zh, go(x, d), y) if axis == 0 else at(zh, x, go(y, d))

    own_slab = pltpu.make_async_copy(x_ref.at[:, 0], sl.at[0, 0], loc_sem.at[0])
    own_slab.start()
    slab_p = {}
    for axis in (0, 1):
        for d in (2, 1, 3):
            k = 3 * axis + d
            cp = remote(x_ref.at[:, 0], sl.at[0, k], ss.at[0, k], sr.at[0, k], along(axis, d))
            cp.start()
            slab_p[k] = cp
    slab_f = {}

    def forward(src, k):
        for group, h, end in ((2, nxt, blocks - 1), (1, prv, 0)):
            cp = remote(src, sl.at[group, k], ss.at[group, k], sr.at[group, k], at(zh, x, y, h))
            if k == 0:
                cp.start()
            else:
                pl.when(g != end)(cp.start)
            slab_f[group, k] = cp

    def gather(group, end):
        slab_f[group, 0].wait_recv()

        @pl.when(g == end)
        def _():
            for k in (2, 5, 1, 4, 3, 6):
                remote(
                    sl.at[group, 0], sl.at[group, k], ss.at[3 - group, k], sr.at[group, k],
                    along((k - 1) // 3, (k - 1) % 3 + 1),
                ).start()

    forward(x_ref.at[:, 0], 0)

    tiles = {}
    locals_ = {}

    def exchange(*chunks):
        for c in chunks:
            axis = c % 2
            for d in (2, 1, 3):
                lt = c * N + go(place[axis], d)
                cp = remote(x_ref.at[:, lt], xb.at[c, d], xs.at[c, d], xr.at[c, d], along(axis, d))
                cp.start()
                tiles[c, d] = cp
            cp = pltpu.make_async_copy(x_ref.at[:, c * N + place[axis]], xb.at[c, 0], loc_sem.at[1 + c])
            cp.start()
            locals_[c] = cp

    exchange(0, 1)
    gather(2, 0)
    gather(1, blocks - 1)
    for k in (1, 4, 3, 6, 2, 5):
        slab_p[k].wait_recv()
        forward(sl.at[0, k], k)
    exchange(2, 3)
    own_slab.wait()

    for k in (0, 1, 4, 3, 6, 2, 5):
        if k:
            slab_f[1, k].wait_recv()
            slab_f[2, k].wait_recv()
        own, nex, pre = [spread(sl.at[r, k].reshape(rows, LANE)[...].astype(F32)) for r in range(3)]
        pad = jnp.zeros((rows, WIDE - 10 * AW), F32)
        wide = jnp.concatenate(nex + pre + [own[1], own[2], pad], axis=1).astype(jnp.bfloat16)
        if k < 4:
            sw[0, pl.ds(k * rows, rows), :] = wide
        if k > 3:
            sw[1, pl.ds((k - 3) * rows, rows), :] = wide
        if k == 0:
            sw[1, pl.ds(0, rows), :] = wide

    per = LANE // N
    fin = per // N
    y_copies, z_copies, z_local = {}, {}, {}

    def multiply(c):
        axis = c % 2
        for d in (1, 2, 3):
            tiles[c, d].wait_recv()
        locals_[c].wait()
        block = xb.at[c].reshape(N * rows, LANE)[...]
        prod = lax.dot_general(block, sw[axis], (((0,), (0,)), ((), ())), preferred_element_type=F32)
        for k in range(N):
            pb[c, k] = prod[k * per:(k + 1) * per].astype(LINK)
        for d in (2, 1, 3):
            cp = remote(
                pb.at[c, go(place[1 - axis], d)], yb.at[c, d - 1], ys.at[c, d - 1], yr.at[c, d - 1], along(1 - axis, d)
            )
            cp.start()
            y_copies[c, d] = cp

    def reduce_y(c):
        for d in (1, 2, 3):
            y_copies[c, d].wait_recv()
        total = pb[c, place[1 - c % 2]].astype(F32)
        for d in range(3):
            total = total + yb[c, d].astype(F32)
        for k in range(N):
            sb[c, k] = total[k * fin:(k + 1) * fin].astype(LINK)
        for d in (2, 1, 3, 0):
            zz = go(zh, d)
            cp = remote(sb.at[c, zz, :, pl.ds(0, OPW)], zop.at[c, d], os_.at[c, d], or_.at[c, d], at(zz, x, y, nxt))
            cp.start()
            z_copies[c, d, 0] = cp
            src = sb.at[c, zz, :, pl.ds(OPW, RESTW)]
            if d == 0:
                cp = pltpu.make_async_copy(src, zrest.at[c, d], rr.at[c, d])
                cp.start()
                z_local[c] = cp
            else:
                cp = remote(src, zrest.at[c, d], rs.at[c, d], rr.at[c, d], at(zz, x, y))
                cp.start()
                z_copies[c, d, 1] = cp

    def reduce_z(c):
        z_local[c].wait()
        for d in range(N):
            z_copies[c, d, 0].wait_recv()
            if d:
                z_copies[c, d, 1].wait_recv()
        first = zop[c, 0].astype(F32)
        second = zrest[c, 0].astype(F32)
        for d in (1, 2, 3):
            first = first + zop[c, d].astype(F32)
            second = second + zrest[c, d].astype(F32)
        tb[pl.ds(c * fin, fin), pl.ds(0, OPW)] = first
        tb[pl.ds(c * fin, fin), pl.ds(OPW, RESTW)] = second

    def run(step, *chunks):
        for c in chunks:
            step(c)

    run(multiply, 0, 1)
    exchange(4, 5)
    run(multiply, 2, 3)
    exchange(6, 7)
    run(reduce_y, 0, 1, 2, 3)
    run(multiply, 4, 5, 6, 7)
    run(reduce_y, 4, 5)
    run(reduce_z, 0, 1, 2, 3)
    run(reduce_y, 6, 7)
    run(reduce_z, 4, 5, 6, 7)

    lane = lax.broadcasted_iota(jnp.int32, (fin, LANE), 1)
    row = lax.broadcasted_iota(jnp.int32, (fin, LANE), 0)
    columns = []
    for c in range(CHUNKS):
        lt = c * N + place[c % 2]
        offset = place[1 - c % 2] * per + zh * fin
        line = jnp.broadcast_to(vir_ref[pl.ds(lt, 1), :], (fin, LANE))
        columns.append(jnp.sum(jnp.where(lane == row + offset, line, 0.0), axis=1, keepdims=True))
    eb = jnp.concatenate(columns, axis=0)
    ea = vir_ref[0:1, 0:AW]
    eo = [occ_ref[2 * g], occ_ref[2 * g + 1]]
    ep = [occ_ref[2 * prv], occ_ref[2 * prv + 1]]

    def amplitude(k, ei, ej):
        return tb[:, k * AW:(k + 1) * AW] / (((ei + ej) - ea) - eb)

    op = [[amplitude(2 * i + j, eo[i], ep[j]) for j in range(2)] for i in range(2)]
    po = [[amplitude(4 + 2 * i + j, ep[i], eo[j]) for j in range(2)] for i in range(2)]
    ow = [amplitude(8, eo[0], eo[1]), amplitude(9, eo[1], eo[0])]
    mop = [[2.0 * op[i][j] - po[j][i] for j in range(2)] for i in range(2)]
    mpo = [[2.0 * po[i][j] - op[j][i] for j in range(2)] for i in range(2)]
    mow = [2.0 * ow[0] - ow[1], 2.0 * ow[1] - ow[0]]
    left = jnp.concatenate(op[0] + op[1] + po[0] + po[1] + ow, axis=0)
    right = jnp.concatenate(mop[0] + mop[1] + mpo[0] + mpo[1] + mow, axis=0)
    vv = lax.dot_general(
        left, right, (((0,), (0,)), ((), ())), preferred_element_type=F32, precision=lax.Precision.HIGHEST
    )

    def inner(a, b):
        return jnp.sum(jnp.sum(a * b, axis=1, keepdims=True), axis=0, keepdims=True)

    oo = []
    for i in range(2):
        for j in range(2):
            s = inner(op[i][0], mop[j][0]) + inner(op[i][1], mop[j][1])
            if i == j:
                s = s + inner(ow[i], mow[i])
            oo.append(s)
    corner = jnp.zeros((AW, LANE - AW), F32)
    cl = lax.broadcasted_iota(jnp.int32, corner.shape, 1)
    for k in range(4):
        corner = jnp.where(cl == k, jnp.broadcast_to(oo[k], corner.shape), corner)
    va[...] = jnp.concatenate([2.0 * vv, -2.0 * corner], axis=1)

    piece = AW // N
    fin_copies = []
    group = []
    for d in (1, 2, 3):
        yy = go(y, d)
        cp = remote(
            va.at[pl.ds(pl.multiple_of(yy * piece, 8), piece)], vb.at[d - 1], vs.at[0, d], vr.at[0, d], at(zh, x, yy)
        )
        cp.start()
        group.append(cp)
    for cp in group:
        cp.wait_recv()
    fin_copies += group
    total = va[pl.ds(pl.multiple_of(y * piece, 8), piece), :]
    for d in range(3):
        total = total + vb[d]

    def everyone(total, buf, stage, me, where):
        buf[me] = total
        group = []
        for d in (1, 2, 3):
            cp = remote(buf.at[me], buf.at[me], vs.at[stage, d], vr.at[stage, d], where(d))
            cp.start()
            group.append(cp)
        for cp in group:
            cp.wait_recv()
        return group

    fin_copies += everyone(total, vc.at[0], 1, x, lambda d: at(zh, go(x, d), y))
    total = (vc[0, 0] + vc[0, 1]) + (vc[0, 2] + vc[0, 3])
    fin_copies += everyone(total, vc.at[1], 2, zh, lambda d: at(go(zh, d), x, y))
    total = (vc[1, 0] + vc[1, 1]) + (vc[1, 2] + vc[1, 3])
    fin_copies += everyone(total, vd, 3, y, lambda d: at(zh, x, go(y, d)))
    for k in range(N):
        out_ref[pl.ds(k * piece, piece), :] = vd[k]

    for group in (slab_p.values(), slab_f.values(), tiles.values(), y_copies.values(), z_copies.values(), fin_copies):
        for cp in group:
            cp.wait_send()


def shards(three_index, occ_energy, vir_energy):
    depth, occ, vir = three_index.shape
    tiles = vir // LANE
    view = three_index.reshape(depth, occ, tiles, LANE).transpose(0, 2, 1, 3)
    bf16 = jnp.bfloat16
    per = LANE // N
    fin = per // N
    piece = AW // N
    dma = pltpu.SemaphoreType.DMA
    out = pl.pallas_call(
        kernel,
        out_shape=jax.ShapeDtypeStruct((AW, LANE), F32),
        in_specs=[
            pl.BlockSpec(memory_space=pl.ANY),
            pl.BlockSpec(memory_space=pltpu.SMEM),
            pl.BlockSpec(memory_space=pltpu.VMEM),
        ],
        out_specs=pl.BlockSpec(memory_space=pltpu.VMEM),
        scratch_shapes=[
            pltpu.VMEM((CHUNKS, N, depth, occ, LANE), bf16),
            pltpu.VMEM((3, 7, depth, occ, LANE), bf16),
            pltpu.VMEM((2, N * depth * occ, WIDE), bf16),
            pltpu.VMEM((CHUNKS, N, per, WIDE), LINK),
            pltpu.VMEM((CHUNKS, 3, per, WIDE), LINK),
            pltpu.VMEM((CHUNKS, N, fin, WIDE), LINK),
            pltpu.VMEM((CHUNKS, N, fin, OPW), LINK),
            pltpu.VMEM((CHUNKS, N, fin, RESTW), LINK),
            pltpu.VMEM((CHUNKS * fin, WIDE), F32),
            pltpu.VMEM((AW, LANE), F32),
            pltpu.VMEM((3, piece, LANE), F32),
            pltpu.VMEM((2, N, piece, LANE), F32),
            pltpu.VMEM((N, piece, LANE), F32),
            dma((1 + CHUNKS,)),
            dma((CHUNKS, N)), dma((CHUNKS, N)),
            dma((3, 7)), dma((3, 7)),
            dma((CHUNKS, 3)), dma((CHUNKS, 3)),
            dma((CHUNKS, N)), dma((CHUNKS, N)),
            dma((CHUNKS, N)), dma((CHUNKS, N)),
            dma((4, N)), dma((4, N)),
        ],
        compiler_params=pltpu.CompilerParams(
            collective_id=0, has_side_effects=True, vmem_limit_bytes=56 * 1024 * 1024
        ),
        cost_estimate=pl.CostEstimate(flops=4_000_000_000, bytes_accessed=8_000_000, transcendentals=0),
    )(view, occ_energy, vir_energy.reshape(vir // LANE, LANE))
    return out[:, :AW], out[0, AW:AW + 4].reshape(2, 2)


def solution(mesh):
    return jax.shard_map(
        shards,
        mesh=mesh,
        in_specs=(P("aux", "blk", None), P(), P()),
        out_specs=(P("blk", None), P("blk", None)),
        check_vma=False,
    )
```

```python
import functools

import jax
import jax.numpy as jnp
from jax import lax
from jax.experimental import pallas as pl
from jax.experimental.pallas import tpu as pltpu
from jax.sharding import PartitionSpec as P

MESH = pl.DeviceIdType.MESH
AW = 96
LANE = 128
CHUNKS = 8
N = 4
WIDE = 1024
OPW = 4 * AW
RESTW = WIDE - OPW
LINK = jnp.bfloat16
F32 = jnp.float32


def spread(raw):
    rows = lax.broadcasted_iota(jnp.int32, raw.shape, 0)
    even = lax.rem(rows, 2) == 0
    zero = jnp.zeros_like(raw)
    up = jnp.concatenate([raw[1:], raw[:1]], axis=0)
    down = jnp.concatenate([raw[-1:], raw[:-1]], axis=0)
    f00 = jnp.where(even, raw, zero)
    f11 = jnp.where(even, zero, raw)
    f10 = jnp.where(even, up, zero)
    f01 = jnp.where(even, zero, down)
    return [f[:, :AW] for f in (f00, f01, f10, f11)]


def kernel(
    x_ref, occ_ref, vir_ref, out_ref,
    xb, sl, sw, pb, yb, sb, zop, zrest, tb, va, vb, vc, vd,
    loc_sem, xs, xr, ss, sr, ys, yr, os_, or_, rs, rr, vs, vr, ready,
):
    g = lax.axis_index("blk")
    aux = lax.axis_index("aux")
    blocks = 8
    zh = aux // 16
    x = lax.rem(aux // 4, 4)
    y = lax.rem(aux, 4)
    nxt, prv = lax.rem(g + 1, blocks), lax.rem(g + blocks - 1, blocks)
    depth = x_ref.shape[0]
    rows = 2 * depth

    def at(z_, x_, y_, g_=None):
        return {"blk": g if g_ is None else g_, "aux": z_ * 16 + x_ * 4 + y_}

    def go(v, d):
        return lax.rem(v + d, N)

    def signal(sem, peer):
        pl.semaphore_signal(sem, inc=1, device_id=peer, device_id_type=MESH)

    def rank(v):
        return v // 2 * 2 + lax.rem(v + v // 2, 2)

    mine = rank(zh)
    barrier = pltpu.get_barrier_semaphore()
    near = [at(zh, go(x, d), y) for d in (2, 1, 3)]
    near += [at(zh, x, go(y, d)) for d in (2, 1, 3)]
    near += [at(zh, x, y, h) for h in (nxt, prv)]
    for peer in near:
        signal(barrier, peer)
    for d in (2, 1, 3):
        @pl.when(rank(go(zh, d)) > mine)
        def _():
            for h in (g, nxt, prv):
                signal(barrier, at(go(zh, d), x, y, h))
    pl.semaphore_wait(barrier, len(near) + 3 * mine)

    def answer():
        for d in (2, 1, 3):
            @pl.when(rank(go(zh, d)) < mine)
            def _():
                for h in (g, prv):
                    signal(ready, at(go(zh, d), x, y, h))

    def remote(src, dst, send, recv, peer):
        return pltpu.make_async_remote_copy(
            src_ref=src, dst_ref=dst, send_sem=send, recv_sem=recv, device_id=peer, device_id_type=MESH
        )

    place = (x, y)

    def along(axis, d):
        return at(zh, go(x, d), y) if axis == 0 else at(zh, x, go(y, d))

    own_slab = pltpu.make_async_copy(x_ref.at[:, 0], sl.at[0, 0], loc_sem.at[0])
    own_slab.start()
    slab_p = {}
    for axis in (0, 1):
        for d in (2, 1, 3):
            k = 3 * axis + d
            cp = remote(x_ref.at[:, 0], sl.at[0, k], ss.at[0, k], sr.at[0, k], along(axis, d))
            cp.start()
            slab_p[k] = cp
    slab_f = {}

    def forward(src, k):
        for group, h, end in ((2, nxt, blocks - 1), (1, prv, 0)):
            cp = remote(src, sl.at[group, k], ss.at[group, k], sr.at[group, k], at(zh, x, y, h))
            if k == 0:
                cp.start()
            else:
                pl.when(g != end)(cp.start)
            slab_f[group, k] = cp

    def gather(group, end):
        slab_f[group, 0].wait_recv()

        @pl.when(g == end)
        def _():
            for k in (2, 5, 1, 4, 3, 6):
                remote(
                    sl.at[group, 0], sl.at[group, k], ss.at[3 - group, k], sr.at[group, k],
                    along((k - 1) // 3, (k - 1) % 3 + 1),
                ).start()

    forward(x_ref.at[:, 0], 0)

    tiles = {}
    locals_ = {}

    def exchange(*chunks):
        for c in chunks:
            axis = c % 2
            for d in (2, 1, 3):
                lt = c * N + go(place[axis], d)
                cp = remote(x_ref.at[:, lt], xb.at[c, d], xs.at[c, d], xr.at[c, d], along(axis, d))
                cp.start()
                tiles[c, d] = cp
            cp = pltpu.make_async_copy(x_ref.at[:, c * N + place[axis]], xb.at[c, 0], loc_sem.at[1 + c])
            cp.start()
            locals_[c] = cp

    exchange(0, 1)
    gather(2, 0)
    gather(1, blocks - 1)
    for k in (1, 4, 3, 6, 2, 5):
        slab_p[k].wait_recv()
        forward(sl.at[0, k], k)
    exchange(2, 3, 4, 5)
    answer()
    own_slab.wait()

    def place_wide(k, start, forms):
        wide = jnp.concatenate(forms, axis=1).astype(jnp.bfloat16)
        for axis in (0, 1):
            if k == 0 or (k - 1) // 3 == axis:
                slot = 0 if k == 0 else k - 3 * axis
                sw[axis, pl.ds(slot * rows, rows), pl.ds(start, wide.shape[1])] = wide

    def forms(group, k):
        return spread(sl.at[group, k].reshape(rows, LANE)[...].astype(F32))

    pad = jnp.zeros((rows, WIDE - 10 * AW), F32)
    for k in range(7):
        own = forms(0, k)
        place_wide(k, 2 * OPW, [own[1], own[2], pad])
    for k in (0, 1, 4, 3, 6, 2, 5):
        for group, start in ((1, 0), (2, OPW)):
            if k:
                slab_f[group, k].wait_recv()
            place_wide(k, start, forms(group, k))

    per = LANE // N
    fin = per // N
    y_copies, z_copies = {}, {}

    def multiply(c):
        axis = c % 2
        for d in (1, 2, 3):
            tiles[c, d].wait_recv()
        locals_[c].wait()
        block = xb.at[c].reshape(N * rows, LANE)[...]
        prod = lax.dot_general(block, sw[axis], (((0,), (0,)), ((), ())), preferred_element_type=F32)
        for k in range(N):
            pb[c, k] = prod[k * per:(k + 1) * per].astype(LINK)
        for d in (2, 1, 3):
            cp = remote(
                pb.at[c, go(place[1 - axis], d)], yb.at[c, d - 1], ys.at[c, d - 1], yr.at[c, d - 1], along(1 - axis, d)
            )
            cp.start()
            y_copies[c, d] = cp

    def reduce_y(pair):
        for c in (2 * pair, 2 * pair + 1):
            for d in (1, 2, 3):
                y_copies[c, d].wait_recv()
            total = pb[c, place[1 - c % 2]].astype(F32)
            for d in range(3):
                total = total + yb[c, d].astype(F32)
            for k in range(N):
                sb[pair, k, c % 2] = total[k * fin:(k + 1) * fin].astype(LINK)
        for d in (2, 1, 3, 0):
            zz = go(zh, d)
            src = sb.at[pair, zz, :, :, pl.ds(0, OPW)]
            cp = remote(src, zop.at[pair, d], os_.at[pair, d], or_.at[pair, d], at(zz, x, y, nxt))
            cp.start()
            z_copies[pair, d, 0] = cp
            if d:
                src = sb.at[pair, zz, :, :, pl.ds(OPW, RESTW)]
                cp = remote(src, zrest.at[pair, d - 1], rs.at[pair, d], rr.at[pair, d], at(zz, x, y))
                cp.start()
                z_copies[pair, d, 1] = cp

    def reduce_z(pair):
        for cp in [z_copies[pair, d, j] for d in (0, 1, 3, 2) for j in (0, 1) if d or not j]:
            cp.wait_recv()
        for j in (0, 1):
            first = zop[pair, 0, j].astype(F32)
            second = sb[pair, zh, j, :, pl.ds(OPW, RESTW)].astype(F32)
            for d in (1, 2, 3):
                first = first + zop[pair, d, j].astype(F32)
                second = second + zrest[pair, d - 1, j].astype(F32)
            part = pl.ds((2 * pair + j) * fin, fin)
            tb[part, pl.ds(0, OPW)] = first
            tb[part, pl.ds(OPW, RESTW)] = second

    def multiply_all(*chunks):
        for c in chunks:
            multiply(c)

    multiply_all(0, 1, 2, 3)
    multiply_all(4, 5)
    exchange(6, 7)

    @pl.when(mine < N - 1)
    def _():
        pl.semaphore_wait(ready, 2 * (N - 1 - mine))

    reduce_y(0)
    reduce_y(1)
    multiply_all(6, 7)
    reduce_y(2)
    reduce_z(0)
    reduce_z(1)
    reduce_y(3)
    reduce_z(2)
    reduce_z(3)

    lane = lax.broadcasted_iota(jnp.int32, (fin, LANE), 1)
    row = lax.broadcasted_iota(jnp.int32, (fin, LANE), 0)
    columns = []
    for c in range(CHUNKS):
        lt = c * N + place[c % 2]
        offset = place[1 - c % 2] * per + zh * fin
        line = jnp.broadcast_to(vir_ref[pl.ds(lt, 1), :], (fin, LANE))
        columns.append(jnp.sum(jnp.where(lane == row + offset, line, 0.0), axis=1, keepdims=True))
    eb = jnp.concatenate(columns, axis=0)
    ea = vir_ref[0:1, 0:AW]
    eo = [occ_ref[2 * g], occ_ref[2 * g + 1]]
    ep = [occ_ref[2 * prv], occ_ref[2 * prv + 1]]

    def amplitude(k, ei, ej):
        return tb[:, k * AW:(k + 1) * AW] / (((ei + ej) - ea) - eb)

    op = [[amplitude(2 * i + j, eo[i], ep[j]) for j in range(2)] for i in range(2)]
    po = [[amplitude(4 + 2 * i + j, ep[i], eo[j]) for j in range(2)] for i in range(2)]
    ow = [amplitude(8, eo[0], eo[1]), amplitude(9, eo[1], eo[0])]
    mop = [[2.0 * op[i][j] - po[j][i] for j in range(2)] for i in range(2)]
    mpo = [[2.0 * po[i][j] - op[j][i] for j in range(2)] for i in range(2)]
    mow = [2.0 * ow[0] - ow[1], 2.0 * ow[1] - ow[0]]
    left = jnp.concatenate(op[0] + op[1] + po[0] + po[1] + ow, axis=0)
    right = jnp.concatenate(mop[0] + mop[1] + mpo[0] + mpo[1] + mow, axis=0)
    vv = lax.dot_general(
        left, right, (((0,), (0,)), ((), ())), preferred_element_type=F32, precision=lax.Precision.HIGHEST
    )

    def inner(a, b):
        return jnp.sum(jnp.sum(a * b, axis=1, keepdims=True), axis=0, keepdims=True)

    oo = []
    for i in range(2):
        for j in range(2):
            s = inner(op[i][0], mop[j][0]) + inner(op[i][1], mop[j][1])
            if i == j:
                s = s + inner(ow[i], mow[i])
            oo.append(s)
    corner = jnp.zeros((AW, LANE - AW), F32)
    cl = lax.broadcasted_iota(jnp.int32, corner.shape, 1)
    cr = lax.broadcasted_iota(jnp.int32, corner.shape, 0)
    for k in range(4):
        here = jnp.logical_and(cr == k // 2, cl == k % 2)
        corner = jnp.where(here, jnp.broadcast_to(oo[k], corner.shape), corner)
    va[...] = jnp.concatenate([2.0 * vv, -2.0 * corner], axis=1)

    piece = AW // N
    fin_copies = []
    group = []
    for d in (1, 2, 3):
        yy = go(y, d)
        cp = remote(
            va.at[pl.ds(pl.multiple_of(yy * piece, 8), piece)], vb.at[d - 1], vs.at[0, d], vr.at[0, d], at(zh, x, yy)
        )
        cp.start()
        group.append(cp)
    for cp in group:
        cp.wait_recv()
    fin_copies += group
    total = va[pl.ds(pl.multiple_of(y * piece, 8), piece), :]
    for d in range(3):
        total = total + vb[d]

    def everyone(total, buf, stage, me, where, meanwhile=()):
        buf[me] = total
        group = []
        for d in (2, 1, 3):
            cp = remote(buf.at[me], buf.at[me], vs.at[stage, d], vr.at[stage, d], where(d))
            cp.start()
            group.append(cp)
        for copies in meanwhile:
            for cp in copies:
                cp.wait_send()
        for cp in group:
            cp.wait_recv()
        return group

    fin_copies += everyone(total, vc.at[0], 1, x, lambda d: at(zh, go(x, d), y), (slab_p.values(), slab_f.values()))
    total = (vc[0, 0] + vc[0, 1]) + (vc[0, 2] + vc[0, 3])
    fin_copies += everyone(
        total, vc.at[1], 2, zh, lambda d: at(go(zh, d), x, y), (tiles.values(), y_copies.values(), z_copies.values())
    )
    total = (vc[1, 0] + vc[1, 1]) + (vc[1, 2] + vc[1, 3])
    fin_copies += everyone(total, vd, 3, y, lambda d: at(zh, x, go(y, d)))
    for k in range(N):
        out_ref[pl.ds(k * piece, piece), :] = vd[k]
    out_ref[pl.ds(AW, 8), :] = jnp.concatenate([vd[0][0:8, AW:]] * 4, axis=1)
    for cp in fin_copies:
        cp.wait_send()


def shards(three_index, occ_energy, vir_energy):
    depth, occ, vir = three_index.shape
    tiles = vir // LANE
    view = three_index.reshape(depth, occ, tiles, LANE).transpose(0, 2, 1, 3)
    bf16 = jnp.bfloat16
    per = LANE // N
    fin = per // N
    piece = AW // N
    dma = pltpu.SemaphoreType.DMA
    out = pl.pallas_call(
        kernel,
        out_shape=jax.ShapeDtypeStruct((AW + 8, LANE), F32),
        in_specs=[
            pl.BlockSpec(memory_space=pl.ANY),
            pl.BlockSpec(memory_space=pltpu.SMEM),
            pl.BlockSpec(memory_space=pltpu.VMEM),
        ],
        out_specs=pl.BlockSpec(memory_space=pltpu.VMEM),
        scratch_shapes=[
            pltpu.VMEM((CHUNKS, N, depth, occ, LANE), bf16),
            pltpu.VMEM((3, 7, depth, occ, LANE), bf16),
            pltpu.VMEM((2, N * depth * occ, WIDE), bf16),
            pltpu.VMEM((CHUNKS, N, per, WIDE), LINK),
            pltpu.VMEM((CHUNKS, 3, per, WIDE), LINK),
            pltpu.VMEM((CHUNKS // 2, N, 2, fin, WIDE), LINK),
            pltpu.VMEM((CHUNKS // 2, N, 2, fin, OPW), LINK),
            pltpu.VMEM((CHUNKS // 2, 3, 2, fin, RESTW), LINK),
            pltpu.VMEM((CHUNKS * fin, WIDE), F32),
            pltpu.VMEM((AW, LANE), F32),
            pltpu.VMEM((3, piece, LANE), F32),
            pltpu.VMEM((2, N, piece, LANE), F32),
            pltpu.VMEM((N, piece, LANE), F32),
            dma((1 + CHUNKS,)),
            dma((CHUNKS, N)), dma((CHUNKS, N)),
            dma((3, 7)), dma((3, 7)),
            dma((CHUNKS, 3)), dma((CHUNKS, 3)),
            dma((CHUNKS // 2, N)), dma((CHUNKS // 2, N)),
            dma((CHUNKS // 2, N)), dma((CHUNKS // 2, N)),
            dma((4, N)), dma((4, N)),
            pltpu.SemaphoreType.REGULAR,
        ],
        compiler_params=pltpu.CompilerParams(
            collective_id=0, has_side_effects=True, vmem_limit_bytes=56 * 1024 * 1024
        ),
        cost_estimate=pl.CostEstimate(flops=4_000_000_000, bytes_accessed=8_000_000, transcendentals=0),
    )(view, occ_energy, vir_energy.reshape(vir // LANE, LANE))
    return out[:AW, :AW], out[AW:AW + 2, :2]


def solution(mesh):
    return jax.shard_map(
        shards,
        mesh=mesh,
        in_specs=(P("aux", "blk", None), P(), P()),
        out_specs=(P("blk", None), P("blk", None)),
        check_vma=False,
    )
```

```python
import functools

import jax
import jax.numpy as jnp
from jax import lax
from jax.experimental import pallas as pl
from jax.experimental.pallas import tpu as pltpu
from jax.sharding import PartitionSpec as P

MESH = pl.DeviceIdType.MESH
AW = 96
LANE = 128
CHUNKS = 8
N = 4
WIDE = 1024
OPW = 4 * AW
RESTW = WIDE - OPW
LINK = jnp.bfloat16
F32 = jnp.float32


def spread(raw):
    rows = lax.broadcasted_iota(jnp.int32, raw.shape, 0)
    even = lax.rem(rows, 2) == 0
    zero = jnp.zeros_like(raw)
    up = jnp.concatenate([raw[1:], raw[:1]], axis=0)
    down = jnp.concatenate([raw[-1:], raw[:-1]], axis=0)
    f00 = jnp.where(even, raw, zero)
    f11 = jnp.where(even, zero, raw)
    f10 = jnp.where(even, up, zero)
    f01 = jnp.where(even, zero, down)
    return [f[:, :AW] for f in (f00, f01, f10, f11)]


def kernel(
    x_ref, occ_ref, vir_ref, out_ref,
    xb, sl, sw, pb, yb, sb, zop, zrest, tb, va, vb, vc, vd,
    loc_sem, xs, xr, ss, sr, ys, yr, os_, or_, rs, rr, vs, vr, ready,
):
    g = lax.axis_index("blk")
    aux = lax.axis_index("aux")
    blocks = 8
    zh = aux // 16
    x = lax.rem(aux // 4, 4)
    y = lax.rem(aux, 4)
    nxt, prv = lax.rem(g + 1, blocks), lax.rem(g + blocks - 1, blocks)
    depth = x_ref.shape[0]
    rows = 2 * depth

    def at(z_, x_, y_, g_=None):
        return {"blk": g if g_ is None else g_, "aux": z_ * 16 + x_ * 4 + y_}

    def go(v, d):
        return lax.rem(v + d, N)

    def signal(sem, peer):
        pl.semaphore_signal(sem, inc=1, device_id=peer, device_id_type=MESH)

    def rank(v):
        return v // 2 * 2 + lax.rem(v + v // 2, 2)

    mine = rank(zh)
    barrier = pltpu.get_barrier_semaphore()
    near = [at(zh, go(x, d), y) for d in (2, 1, 3)]
    near += [at(zh, x, go(y, d)) for d in (2, 1, 3)]
    near += [at(zh, x, y, h) for h in (nxt, prv)]
    for peer in near:
        signal(barrier, peer)
    for d in (2, 1, 3):
        @pl.when(rank(go(zh, d)) > mine)
        def _():
            for h in (g, nxt, prv):
                signal(barrier, at(go(zh, d), x, y, h))
    pl.semaphore_wait(barrier, len(near) + 3 * mine)

    def answer():
        for d in (2, 1, 3):
            @pl.when(rank(go(zh, d)) < mine)
            def _():
                for h in (g, prv):
                    signal(ready, at(go(zh, d), x, y, h))

    def remote(src, dst, send, recv, peer):
        return pltpu.make_async_remote_copy(
            src_ref=src, dst_ref=dst, send_sem=send, recv_sem=recv, device_id=peer, device_id_type=MESH
        )

    place = (x, y)

    def along(axis, d):
        return at(zh, go(x, d), y) if axis == 0 else at(zh, x, go(y, d))

    own_slab = pltpu.make_async_copy(x_ref.at[:, 0], sl.at[0, 0], loc_sem.at[0])
    own_slab.start()
    slab_p = {}
    for axis in (0, 1):
        for d in (2, 1, 3):
            k = 3 * axis + d
            cp = remote(x_ref.at[:, 0], sl.at[0, k], ss.at[0, k], sr.at[0, k], along(axis, d))
            cp.start()
            slab_p[k] = cp
    slab_f = {}

    def forward(src, k):
        for group, h, end in ((2, nxt, blocks - 1), (1, prv, 0)):
            cp = remote(src, sl.at[group, k], ss.at[group, k], sr.at[group, k], at(zh, x, y, h))
            if k == 0:
                cp.start()
            else:
                pl.when(g != end)(cp.start)
            slab_f[group, k] = cp

    def gather(group, end):
        slab_f[group, 0].wait_recv()

        @pl.when(g == end)
        def _():
            for k in (2, 5, 1, 4, 3, 6):
                remote(
                    sl.at[group, 0], sl.at[group, k], ss.at[3 - group, k], sr.at[group, k],
                    along((k - 1) // 3, (k - 1) % 3 + 1),
                ).start()

    forward(x_ref.at[:, 0], 0)

    tiles = {}
    locals_ = {}

    def exchange(*chunks):
        for c in chunks:
            axis = c % 2
            for d in (2, 1, 3):
                lt = c * N + go(place[axis], d)
                cp = remote(x_ref.at[:, lt], xb.at[c, d], xs.at[c, d], xr.at[c, d], along(axis, d))
                cp.start()
                tiles[c, d] = cp
            cp = pltpu.make_async_copy(x_ref.at[:, c * N + place[axis]], xb.at[c, 0], loc_sem.at[1 + c])
            cp.start()
            locals_[c] = cp

    exchange(0, 1)
    gather(2, 0)
    gather(1, blocks - 1)
    for k in (1, 4, 3, 6, 2, 5):
        slab_p[k].wait_recv()
        forward(sl.at[0, k], k)
    exchange(2, 3, 4, 5)
    answer()
    own_slab.wait()

    def place_wide(k, start, forms):
        wide = jnp.concatenate(forms, axis=1).astype(jnp.bfloat16)
        for axis in (0, 1):
            if k == 0 or (k - 1) // 3 == axis:
                slot = 0 if k == 0 else k - 3 * axis
                sw[axis, pl.ds(slot * rows, rows), pl.ds(start, wide.shape[1])] = wide

    def forms(group, k):
        return spread(sl.at[group, k].reshape(rows, LANE)[...].astype(F32))

    pad = jnp.zeros((rows, WIDE - 10 * AW), F32)
    for k in range(7):
        own = forms(0, k)
        place_wide(k, 2 * OPW, [own[1], own[2], pad])
    for k in (0, 1, 4, 3, 6, 2, 5):
        for group, start in ((1, 0), (2, OPW)):
            if k:
                slab_f[group, k].wait_recv()
            place_wide(k, start, forms(group, k))

    per = LANE // N
    fin = per // N
    y_copies, z_copies = {}, {}

    def multiply(c):
        axis = c % 2
        for d in (1, 2, 3):
            tiles[c, d].wait_recv()
        locals_[c].wait()
        block = xb.at[c].reshape(N * rows, LANE)[...]
        prod = lax.dot_general(block, sw[axis], (((0,), (0,)), ((), ())), preferred_element_type=F32)
        for k in range(N):
            pb[c, k] = prod[k * per:(k + 1) * per].astype(LINK)
        for d in (2, 1, 3):
            cp = remote(
                pb.at[c, go(place[1 - axis], d)], yb.at[c, d - 1], ys.at[c, d - 1], yr.at[c, d - 1], along(1 - axis, d)
            )
            cp.start()
            y_copies[c, d] = cp

    def reduce_y(pair):
        for c in (2 * pair, 2 * pair + 1):
            for d in (1, 2, 3):
                y_copies[c, d].wait_recv()
            total = pb[c, place[1 - c % 2]].astype(F32)
            for d in range(3):
                total = total + yb[c, d].astype(F32)
            for k in range(N):
                sb[pair, k, c % 2] = total[k * fin:(k + 1) * fin].astype(LINK)
        for d in (2, 1, 3, 0):
            zz = go(zh, d)
            src = sb.at[pair, zz, :, :, pl.ds(0, OPW)]
            cp = remote(src, zop.at[pair, d], os_.at[pair, d], or_.at[pair, d], at(zz, x, y, nxt))
            cp.start()
            z_copies[pair, d, 0] = cp
            if d:
                src = sb.at[pair, zz, :, :, pl.ds(OPW, RESTW)]
                cp = remote(src, zrest.at[pair, d - 1], rs.at[pair, d], rr.at[pair, d], at(zz, x, y))
                cp.start()
                z_copies[pair, d, 1] = cp

    def reduce_z(pair):
        for cp in [z_copies[pair, d, j] for d in (0, 1, 3, 2) for j in (0, 1) if d or not j]:
            cp.wait_recv()
        for j in (0, 1):
            first = zop[pair, 0, j].astype(F32)
            second = sb[pair, zh, j, :, pl.ds(OPW, RESTW)].astype(F32)
            for d in (1, 2, 3):
                first = first + zop[pair, d, j].astype(F32)
                second = second + zrest[pair, d - 1, j].astype(F32)
            part = pl.ds((2 * pair + j) * fin, fin)
            tb[part, pl.ds(0, OPW)] = first
            tb[part, pl.ds(OPW, RESTW)] = second

    def multiply_all(*chunks):
        for c in chunks:
            multiply(c)

    lane = lax.broadcasted_iota(jnp.int32, (fin, LANE), 1)
    row = lax.broadcasted_iota(jnp.int32, (fin, LANE), 0)
    ea = vir_ref[0:1, 0:AW]
    eo = [occ_ref[2 * g], occ_ref[2 * g + 1]]
    ep = [occ_ref[2 * prv], occ_ref[2 * prv + 1]]

    def inner(a, b):
        return jnp.sum(jnp.sum(a * b, axis=1, keepdims=True), axis=0, keepdims=True)

    def densities(start, stop):
        columns = []
        for c in range(start, stop):
            lt = c * N + place[c % 2]
            offset = place[1 - c % 2] * per + zh * fin
            line = jnp.broadcast_to(vir_ref[pl.ds(lt, 1), :], (fin, LANE))
            columns.append(jnp.sum(jnp.where(lane == row + offset, line, 0.0), axis=1, keepdims=True))
        eb = jnp.concatenate(columns, axis=0)

        def amplitude(k, ei, ej):
            return tb[start * fin:stop * fin, k * AW:(k + 1) * AW] / (((ei + ej) - ea) - eb)

        op = [[amplitude(2 * i + j, eo[i], ep[j]) for j in range(2)] for i in range(2)]
        po = [[amplitude(4 + 2 * i + j, ep[i], eo[j]) for j in range(2)] for i in range(2)]
        ow = [amplitude(8, eo[0], eo[1]), amplitude(9, eo[1], eo[0])]
        mop = [[2.0 * op[i][j] - po[j][i] for j in range(2)] for i in range(2)]
        mpo = [[2.0 * po[i][j] - op[j][i] for j in range(2)] for i in range(2)]
        mow = [2.0 * ow[0] - ow[1], 2.0 * ow[1] - ow[0]]
        left = jnp.concatenate(op[0] + op[1] + po[0] + po[1] + ow, axis=0)
        right = jnp.concatenate(mop[0] + mop[1] + mpo[0] + mpo[1] + mow, axis=0)
        vv = lax.dot_general(
            left, right, (((0,), (0,)), ((), ())), preferred_element_type=F32, precision=lax.Precision.HIGHEST
        )
        oo = []
        for i in range(2):
            for j in range(2):
                s = inner(op[i][0], mop[j][0]) + inner(op[i][1], mop[j][1])
                if i == j:
                    s = s + inner(ow[i], mow[i])
                oo.append(s)
        corner = jnp.zeros((AW, LANE - AW), F32)
        cl = lax.broadcasted_iota(jnp.int32, corner.shape, 1)
        cr = lax.broadcasted_iota(jnp.int32, corner.shape, 0)
        for k in range(4):
            here = jnp.logical_and(cr == k // 2, cl == k % 2)
            corner = jnp.where(here, jnp.broadcast_to(oo[k], corner.shape), corner)
        return jnp.concatenate([vv, corner], axis=1)

    multiply_all(0, 1, 2, 3)
    multiply_all(4, 5)
    exchange(6, 7)

    @pl.when(mine < N - 1)
    def _():
        pl.semaphore_wait(ready, 2 * (N - 1 - mine))

    reduce_y(0)
    reduce_y(1)
    reduce_y(2)
    multiply_all(6, 7)
    reduce_y(3)
    reduce_z(0)
    reduce_z(1)
    reduce_z(2)
    va[...] = densities(0, 6)
    reduce_z(3)
    va[...] += densities(6, 8)


    piece = AW // N
    fin_copies = []
    group = []
    for d in (1, 2, 3):
        yy = go(y, d)
        cp = remote(
            va.at[pl.ds(pl.multiple_of(yy * piece, 8), piece)], vb.at[d - 1], vs.at[0, d], vr.at[0, d], at(zh, x, yy)
        )
        cp.start()
        group.append(cp)
    for cp in group:
        cp.wait_recv()
    fin_copies += group
    total = va[pl.ds(pl.multiple_of(y * piece, 8), piece), :]
    for d in range(3):
        total = total + vb[d]

    def everyone(total, buf, stage, me, where, meanwhile=()):
        buf[me] = total
        group = []
        for d in (2, 1, 3):
            cp = remote(buf.at[me], buf.at[me], vs.at[stage, d], vr.at[stage, d], where(d))
            cp.start()
            group.append(cp)
        for copies in meanwhile:
            for cp in copies:
                cp.wait_send()
        for cp in group:
            cp.wait_recv()
        return group

    fin_copies += everyone(total, vc.at[0], 1, x, lambda d: at(zh, go(x, d), y), (slab_p.values(), slab_f.values()))
    total = (vc[0, 0] + vc[0, 1]) + (vc[0, 2] + vc[0, 3])
    fin_copies += everyone(
        total, vc.at[1], 2, zh, lambda d: at(go(zh, d), x, y), (tiles.values(), y_copies.values(), z_copies.values())
    )
    total = (vc[1, 0] + vc[1, 1]) + (vc[1, 2] + vc[1, 3])
    fin_copies += everyone(total, vd, 3, y, lambda d: at(zh, x, go(y, d)))
    for k in range(N):
        out_ref[pl.ds(k * piece, piece), :] = vd[k]
    out_ref[pl.ds(AW, 8), :] = jnp.concatenate([vd[0][0:8, AW:]] * 4, axis=1)
    for cp in fin_copies:
        cp.wait_send()


def shards(three_index, occ_energy, vir_energy):
    depth, occ, vir = three_index.shape
    tiles = vir // LANE
    view = three_index.reshape(depth, occ, tiles, LANE).transpose(0, 2, 1, 3)
    bf16 = jnp.bfloat16
    per = LANE // N
    fin = per // N
    piece = AW // N
    dma = pltpu.SemaphoreType.DMA
    out = pl.pallas_call(
        kernel,
        out_shape=jax.ShapeDtypeStruct((AW + 8, LANE), F32),
        in_specs=[
            pl.BlockSpec(memory_space=pl.ANY),
            pl.BlockSpec(memory_space=pltpu.SMEM),
            pl.BlockSpec(memory_space=pltpu.VMEM),
        ],
        out_specs=pl.BlockSpec(memory_space=pltpu.VMEM),
        scratch_shapes=[
            pltpu.VMEM((CHUNKS, N, depth, occ, LANE), bf16),
            pltpu.VMEM((3, 7, depth, occ, LANE), bf16),
            pltpu.VMEM((2, N * depth * occ, WIDE), bf16),
            pltpu.VMEM((CHUNKS, N, per, WIDE), LINK),
            pltpu.VMEM((CHUNKS, 3, per, WIDE), LINK),
            pltpu.VMEM((CHUNKS // 2, N, 2, fin, WIDE), LINK),
            pltpu.VMEM((CHUNKS // 2, N, 2, fin, OPW), LINK),
            pltpu.VMEM((CHUNKS // 2, 3, 2, fin, RESTW), LINK),
            pltpu.VMEM((CHUNKS * fin, WIDE), F32),
            pltpu.VMEM((AW, LANE), F32),
            pltpu.VMEM((3, piece, LANE), F32),
            pltpu.VMEM((2, N, piece, LANE), F32),
            pltpu.VMEM((N, piece, LANE), F32),
            dma((1 + CHUNKS,)),
            dma((CHUNKS, N)), dma((CHUNKS, N)),
            dma((3, 7)), dma((3, 7)),
            dma((CHUNKS, 3)), dma((CHUNKS, 3)),
            dma((CHUNKS // 2, N)), dma((CHUNKS // 2, N)),
            dma((CHUNKS // 2, N)), dma((CHUNKS // 2, N)),
            dma((4, N)), dma((4, N)),
            pltpu.SemaphoreType.REGULAR,
        ],
        compiler_params=pltpu.CompilerParams(
            collective_id=0, has_side_effects=True, vmem_limit_bytes=56 * 1024 * 1024
        ),
        cost_estimate=pl.CostEstimate(flops=4_000_000_000, bytes_accessed=8_000_000, transcendentals=0),
    )(view, occ_energy, vir_energy.reshape(vir // LANE, LANE))
    return 2.0 * out[:AW, :AW], -2.0 * out[AW:AW + 2, :2]


def solution(mesh):
    return jax.shard_map(
        shards,
        mesh=mesh,
        in_specs=(P("aux", "blk", None), P(), P()),
        out_specs=(P("blk", None), P("blk", None)),
        check_vma=False,
    )
```

```python
import functools

import jax
import jax.numpy as jnp
from jax import lax
from jax.experimental import pallas as pl
from jax.experimental.pallas import tpu as pltpu
from jax.sharding import PartitionSpec as P

MESH = pl.DeviceIdType.MESH
AW = 96
LANE = 128
CHUNKS = 8
N = 4
WIDE = 1024
OPW = 4 * AW
RESTW = WIDE - OPW
LINK = jnp.bfloat16
F32 = jnp.float32


def spread(raw):
    rows = lax.broadcasted_iota(jnp.int32, raw.shape, 0)
    even = lax.rem(rows, 2) == 0
    zero = jnp.zeros_like(raw)
    up = jnp.concatenate([raw[1:], raw[:1]], axis=0)
    down = jnp.concatenate([raw[-1:], raw[:-1]], axis=0)
    f00 = jnp.where(even, raw, zero)
    f11 = jnp.where(even, zero, raw)
    f10 = jnp.where(even, up, zero)
    f01 = jnp.where(even, zero, down)
    return [f[:, :AW] for f in (f00, f01, f10, f11)]


def kernel(
    x_ref, occ_ref, vir_ref, out_ref,
    xb, sl, sw, pb, yb, sb, zop, zrest, tb, va, vb, vc, vd,
    loc_sem, xs, xr, ss, sr, ys, yr, os_, or_, rs, rr, vs, vr, ready,
):
    g = lax.axis_index("blk")
    aux = lax.axis_index("aux")
    blocks = 8
    zh = aux // 16
    x = lax.rem(aux // 4, 4)
    y = lax.rem(aux, 4)
    nxt, prv = lax.rem(g + 1, blocks), lax.rem(g + blocks - 1, blocks)
    depth = x_ref.shape[0]
    rows = 2 * depth

    def at(z_, x_, y_, g_=None):
        return {"blk": g if g_ is None else g_, "aux": z_ * 16 + x_ * 4 + y_}

    def go(v, d):
        return lax.rem(v + d, N)

    def signal(sem, peer):
        pl.semaphore_signal(sem, inc=1, device_id=peer, device_id_type=MESH)

    def rank(v):
        return v // 2 * 2 + lax.rem(v + v // 2, 2)

    mine = rank(zh)
    barrier = pltpu.get_barrier_semaphore()
    near = [at(zh, go(x, d), y) for d in (2, 1, 3)]
    near += [at(zh, x, go(y, d)) for d in (2, 1, 3)]
    near += [at(zh, x, y, h) for h in (nxt, prv)]
    for peer in near:
        signal(barrier, peer)
    for d in (2, 1, 3):
        @pl.when(rank(go(zh, d)) > mine)
        def _():
            for h in (g, nxt, prv):
                signal(barrier, at(go(zh, d), x, y, h))
    pl.semaphore_wait(barrier, len(near) + 3 * mine)

    def answer():
        for d in (2, 1, 3):
            @pl.when(rank(go(zh, d)) < mine)
            def _():
                for h in (g, prv):
                    signal(ready, at(go(zh, d), x, y, h))

    def remote(src, dst, send, recv, peer):
        return pltpu.make_async_remote_copy(
            src_ref=src, dst_ref=dst, send_sem=send, recv_sem=recv, device_id=peer, device_id_type=MESH
        )

    place = (x, y)

    def along(axis, d):
        return at(zh, go(x, d), y) if axis == 0 else at(zh, x, go(y, d))

    own_slab = pltpu.make_async_copy(x_ref.at[:, 0], sl.at[0, 0], loc_sem.at[0])
    own_slab.start()
    slab_p = {}
    for axis in (0, 1):
        for d in (2, 1, 3):
            k = 3 * axis + d
            cp = remote(x_ref.at[:, 0], sl.at[0, k], ss.at[0, k], sr.at[0, k], along(axis, d))
            cp.start()
            slab_p[k] = cp
    slab_f = {}

    def forward(src, k):
        for group, h, end in ((2, nxt, blocks - 1), (1, prv, 0)):
            cp = remote(src, sl.at[group, k], ss.at[group, k], sr.at[group, k], at(zh, x, y, h))
            if k == 0:
                cp.start()
            else:
                pl.when(g != end)(cp.start)
            slab_f[group, k] = cp

    def gather(group, end):
        slab_f[group, 0].wait_recv()

        @pl.when(g == end)
        def _():
            for k in (2, 5, 1, 4, 3, 6):
                remote(
                    sl.at[group, 0], sl.at[group, k], ss.at[3 - group, k], sr.at[group, k],
                    along((k - 1) // 3, (k - 1) % 3 + 1),
                ).start()

    forward(x_ref.at[:, 0], 0)

    tiles = {}
    locals_ = {}

    def exchange(*chunks):
        for c in chunks:
            axis = c % 2
            for d in (2, 1, 3):
                lt = c * N + go(place[axis], d)
                cp = remote(x_ref.at[:, lt], xb.at[c, d], xs.at[c, d], xr.at[c, d], along(axis, d))
                cp.start()
                tiles[c, d] = cp
            cp = pltpu.make_async_copy(x_ref.at[:, c * N + place[axis]], xb.at[c, 0], loc_sem.at[1 + c])
            cp.start()
            locals_[c] = cp

    exchange(0, 1)
    for k in (1, 4, 3, 6, 2, 5):
        if k == 2:
            gather(2, 0)
            gather(1, blocks - 1)
        slab_p[k].wait_recv()
        forward(sl.at[0, k], k)
    exchange(2, 3, 4, 5)
    answer()
    own_slab.wait()

    def place_wide(k, start, forms):
        wide = jnp.concatenate(forms, axis=1).astype(jnp.bfloat16)
        for axis in (0, 1):
            if k == 0 or (k - 1) // 3 == axis:
                slot = 0 if k == 0 else k - 3 * axis
                sw[axis, pl.ds(slot * rows, rows), pl.ds(start, wide.shape[1])] = wide

    def forms(group, k):
        return spread(sl.at[group, k].reshape(rows, LANE)[...].astype(F32))

    pad = jnp.zeros((rows, WIDE - 10 * AW), F32)
    for k in range(7):
        own = forms(0, k)
        place_wide(k, 2 * OPW, [own[1], own[2], pad])
    for k in (0, 1, 4, 3, 6, 2, 5):
        for group, start in ((1, 0), (2, OPW)):
            if k:
                slab_f[group, k].wait_recv()
            place_wide(k, start, forms(group, k))

    per = LANE // N
    fin = per // N
    y_copies, z_copies = {}, {}

    def multiply(c):
        axis = c % 2
        for d in (1, 2, 3):
            tiles[c, d].wait_recv()
        locals_[c].wait()
        block = xb.at[c].reshape(N * rows, LANE)[...]
        prod = lax.dot_general(block, sw[axis], (((0,), (0,)), ((), ())), preferred_element_type=F32)
        for k in range(N):
            pb[c, k] = prod[k * per:(k + 1) * per].astype(LINK)
        for d in (2, 1, 3):
            cp = remote(
                pb.at[c, go(place[1 - axis], d)], yb.at[c, d - 1], ys.at[c, d - 1], yr.at[c, d - 1], along(1 - axis, d)
            )
            cp.start()
            y_copies[c, d] = cp

    def reduce_y(pair):
        for c in (2 * pair, 2 * pair + 1):
            for d in (1, 2, 3):
                y_copies[c, d].wait_recv()
            total = pb[c, place[1 - c % 2]].astype(F32)
            for d in range(3):
                total = total + yb[c, d].astype(F32)
            for k in range(N):
                sb[pair, k, c % 2] = total[k * fin:(k + 1) * fin].astype(LINK)
            if pair == CHUNKS // 2 - 1:
                send_z(pair, pair + c % 2, c % 2)
        if pair < CHUNKS // 2 - 1:
            send_z(pair, pair, slice(None))

    def send_z(pair, sem, j):
        for d in (2, 1, 3, 0):
            zz = go(zh, d)
            src = sb.at[pair, zz, j, :, pl.ds(0, OPW)]
            cp = remote(src, zop.at[pair, d, j], os_.at[sem, d], or_.at[sem, d], at(zz, x, y, nxt))
            cp.start()
            z_copies[pair, sem, d, 0] = cp
            if d:
                src = sb.at[pair, zz, j, :, pl.ds(OPW, RESTW)]
                cp = remote(src, zrest.at[pair, d - 1, j], rs.at[sem, d], rr.at[sem, d], at(zz, x, y))
                cp.start()
                z_copies[pair, sem, d, 1] = cp

    def reduce_z(pair):
        for cp in [cp for key, cp in z_copies.items() if key[0] == pair]:
            cp.wait_recv()
        for j in (0, 1):
            first = zop[pair, 0, j].astype(F32)
            second = sb[pair, zh, j, :, pl.ds(OPW, RESTW)].astype(F32)
            for d in (1, 2, 3):
                first = first + zop[pair, d, j].astype(F32)
                second = second + zrest[pair, d - 1, j].astype(F32)
            part = pl.ds((2 * pair + j) * fin, fin)
            tb[part, pl.ds(0, OPW)] = first
            tb[part, pl.ds(OPW, RESTW)] = second

    def multiply_all(*chunks):
        for c in chunks:
            multiply(c)

    lane = lax.broadcasted_iota(jnp.int32, (fin, LANE), 1)
    row = lax.broadcasted_iota(jnp.int32, (fin, LANE), 0)
    ea = vir_ref[0:1, 0:AW]
    eo = [occ_ref[2 * g], occ_ref[2 * g + 1]]
    ep = [occ_ref[2 * prv], occ_ref[2 * prv + 1]]

    def inner(a, b):
        return jnp.sum(jnp.sum(a * b, axis=1, keepdims=True), axis=0, keepdims=True)

    def densities(start, stop):
        columns = []
        for c in range(start, stop):
            lt = c * N + place[c % 2]
            offset = place[1 - c % 2] * per + zh * fin
            line = jnp.broadcast_to(vir_ref[pl.ds(lt, 1), :], (fin, LANE))
            columns.append(jnp.sum(jnp.where(lane == row + offset, line, 0.0), axis=1, keepdims=True))
        eb = jnp.concatenate(columns, axis=0)

        def amplitude(k, ei, ej):
            return tb[start * fin:stop * fin, k * AW:(k + 1) * AW] / (((ei + ej) - ea) - eb)

        op = [[amplitude(2 * i + j, eo[i], ep[j]) for j in range(2)] for i in range(2)]
        po = [[amplitude(4 + 2 * i + j, ep[i], eo[j]) for j in range(2)] for i in range(2)]
        ow = [amplitude(8, eo[0], eo[1]), amplitude(9, eo[1], eo[0])]
        mop = [[2.0 * op[i][j] - po[j][i] for j in range(2)] for i in range(2)]
        mpo = [[2.0 * po[i][j] - op[j][i] for j in range(2)] for i in range(2)]
        mow = [2.0 * ow[0] - ow[1], 2.0 * ow[1] - ow[0]]
        left = jnp.concatenate(op[0] + op[1] + po[0] + po[1] + ow, axis=0)
        right = jnp.concatenate(mop[0] + mop[1] + mpo[0] + mpo[1] + mow, axis=0)
        vv = lax.dot_general(
            left, right, (((0,), (0,)), ((), ())), preferred_element_type=F32, precision=lax.Precision.HIGHEST
        )
        oo = []
        for i in range(2):
            for j in range(2):
                s = inner(op[i][0], mop[j][0]) + inner(op[i][1], mop[j][1])
                if i == j:
                    s = s + inner(ow[i], mow[i])
                oo.append(s)
        corner = jnp.zeros((AW, LANE - AW), F32)
        cl = lax.broadcasted_iota(jnp.int32, corner.shape, 1)
        cr = lax.broadcasted_iota(jnp.int32, corner.shape, 0)
        for k in range(4):
            here = jnp.logical_and(cr == k // 2, cl == k % 2)
            corner = jnp.where(here, jnp.broadcast_to(oo[k], corner.shape), corner)
        return jnp.concatenate([vv, corner], axis=1)

    multiply_all(0, 1, 2, 3)
    multiply_all(4, 5)
    exchange(6, 7)

    @pl.when(mine < N - 1)
    def _():
        pl.semaphore_wait(ready, 2 * (N - 1 - mine))

    reduce_y(0)
    reduce_y(1)
    reduce_y(2)
    multiply_all(6, 7)
    reduce_y(3)
    reduce_z(0)
    reduce_z(1)
    reduce_z(2)
    va[...] = densities(0, 6)
    reduce_z(3)
    va[...] += densities(6, 8)


    piece = AW // N
    fin_copies = []
    group = []
    for d in (1, 2, 3):
        yy = go(y, d)
        cp = remote(
            va.at[pl.ds(pl.multiple_of(yy * piece, 8), piece)], vb.at[d - 1], vs.at[0, d], vr.at[0, d], at(zh, x, yy)
        )
        cp.start()
        group.append(cp)
    for cp in group:
        cp.wait_recv()
    fin_copies += group
    total = va[pl.ds(pl.multiple_of(y * piece, 8), piece), :]
    for d in range(3):
        total = total + vb[d]

    def everyone(total, buf, stage, me, where, meanwhile=()):
        buf[me] = total
        group = []
        for d in (2, 1, 3):
            cp = remote(buf.at[me], buf.at[me], vs.at[stage, d], vr.at[stage, d], where(d))
            cp.start()
            group.append(cp)
        for copies in meanwhile:
            for cp in copies:
                cp.wait_send()
        for cp in group:
            cp.wait_recv()
        return group

    fin_copies += everyone(total, vc.at[0], 1, x, lambda d: at(zh, go(x, d), y), (slab_p.values(), slab_f.values()))
    total = (vc[0, 0] + vc[0, 1]) + (vc[0, 2] + vc[0, 3])
    fin_copies += everyone(
        total, vc.at[1], 2, zh, lambda d: at(go(zh, d), x, y), (tiles.values(), y_copies.values(), z_copies.values())
    )
    total = (vc[1, 0] + vc[1, 1]) + (vc[1, 2] + vc[1, 3])
    fin_copies += everyone(total, vd, 3, y, lambda d: at(zh, x, go(y, d)))
    for k in range(N):
        out_ref[pl.ds(k * piece, piece), :] = vd[k]
    out_ref[pl.ds(AW, 8), :] = jnp.concatenate([vd[0][0:8, AW:]] * 4, axis=1)
    for cp in fin_copies:
        cp.wait_send()


def shards(three_index, occ_energy, vir_energy):
    depth, occ, vir = three_index.shape
    tiles = vir // LANE
    view = three_index.reshape(depth, occ, tiles, LANE).transpose(0, 2, 1, 3)
    bf16 = jnp.bfloat16
    per = LANE // N
    fin = per // N
    piece = AW // N
    dma = pltpu.SemaphoreType.DMA
    out = pl.pallas_call(
        kernel,
        out_shape=jax.ShapeDtypeStruct((AW + 8, LANE), F32),
        in_specs=[
            pl.BlockSpec(memory_space=pl.ANY),
            pl.BlockSpec(memory_space=pltpu.SMEM),
            pl.BlockSpec(memory_space=pltpu.VMEM),
        ],
        out_specs=pl.BlockSpec(memory_space=pltpu.VMEM),
        scratch_shapes=[
            pltpu.VMEM((CHUNKS, N, depth, occ, LANE), bf16),
            pltpu.VMEM((3, 7, depth, occ, LANE), bf16),
            pltpu.VMEM((2, N * depth * occ, WIDE), bf16),
            pltpu.VMEM((CHUNKS, N, per, WIDE), LINK),
            pltpu.VMEM((CHUNKS, 3, per, WIDE), LINK),
            pltpu.VMEM((CHUNKS // 2, N, 2, fin, WIDE), LINK),
            pltpu.VMEM((CHUNKS // 2, N, 2, fin, OPW), LINK),
            pltpu.VMEM((CHUNKS // 2, 3, 2, fin, RESTW), LINK),
            pltpu.VMEM((CHUNKS * fin, WIDE), F32),
            pltpu.VMEM((AW, LANE), F32),
            pltpu.VMEM((3, piece, LANE), F32),
            pltpu.VMEM((2, N, piece, LANE), F32),
            pltpu.VMEM((N, piece, LANE), F32),
            dma((1 + CHUNKS,)),
            dma((CHUNKS, N)), dma((CHUNKS, N)),
            dma((3, 7)), dma((3, 7)),
            dma((CHUNKS, 3)), dma((CHUNKS, 3)),
            dma((CHUNKS // 2 + 1, N)), dma((CHUNKS // 2 + 1, N)),
            dma((CHUNKS // 2 + 1, N)), dma((CHUNKS // 2 + 1, N)),
            dma((4, N)), dma((4, N)),
            pltpu.SemaphoreType.REGULAR,
        ],
        compiler_params=pltpu.CompilerParams(
            collective_id=0, has_side_effects=True, vmem_limit_bytes=56 * 1024 * 1024
        ),
        cost_estimate=pl.CostEstimate(flops=4_000_000_000, bytes_accessed=8_000_000, transcendentals=0),
    )(view, occ_energy, vir_energy.reshape(vir // LANE, LANE))
    return 2.0 * out[:AW, :AW], -2.0 * out[AW:AW + 2, :2]


def solution(mesh):
    return jax.shard_map(
        shards,
        mesh=mesh,
        in_specs=(P("aux", "blk", None), P(), P()),
        out_specs=(P("blk", None), P("blk", None)),
        check_vma=False,
    )
```
